512 devices in a mesh: blk: 64 (over z, y_hi, core), rhs: 8 (over y_lo, x).
Axes of the slice: x: 4, y: 8 (y_hi: 4, y_lo: 2; y = y_hi * 2 + y_lo), z: 8, core: 2. Of those that a mesh axis runs over, the one named last changes fastest.
Arguments:
- diag_inverse: float32 [64, 512, 512], P('blk', 'rhs'), may hold values from -2 to 2
- coupling: float32 [64, 512, 512], P('blk', 'rhs'), may hold values from -2 to 2
- rhs_t: float32 [512, 32768], P('rhs', 'blk'), may hold values from -2.4 to 2.4
- prior: float32 [512, 512], P('rhs'), may hold values from -6 to 6
- border_factor: float32 [2048, 32768], P('rhs', 'blk'), may hold values from -0.03125 to 0.03125
- border_rhs: float32 [512, 2048], P('rhs'), may hold values from -6 to 6
Outputs:
- solution: float32 [512, 32768], P('rhs', 'blk')
- border_out: float32 [512, 2048], P('rhs')
The draws below stay inside these ranges and needn't reach their ends.
All inputs are finite; a program needn't handle non-finite values.
Results may differ from the reference program's by a relative error of at most 0.0003.
Values sent between devices are 32-bit elements; how exact they have to be, the bound alone decides.
No kernel may reach another device: no remote copies, remote signals or barrier semaphores. Data moves between devices by JAX's collectives and lax.ppermute only.
A program may use at most 192 MiB of HBM per device.

```python
import math
import jax
import jax.numpy as jnp
from jax import lax

NB = 512
RHS = 512
BORDER = 2048
NBLK = 64
N = 32768


def draw_diag_inverse(key, part):
    key = jax.random.fold_in(key, 11)
    first_key, second_key = jax.random.split(key)
    diagonal = jnp.exp(jax.random.uniform(first_key, (NBLK, NB), jnp.float32, -0.3, 0.2) / NBLK)
    noise = jax.random.normal(second_key, (NBLK, NB, NB), jnp.float32)
    lower = jnp.tril(noise, -1) * (0.2 / math.sqrt(NB))
    return lower + diagonal[:, :, None] * jnp.eye(NB, dtype=jnp.float32)


def draw_coupling(key, part):
    key = jax.random.fold_in(key, 23)
    keys = jax.random.split(key, 6)
    share = 0.5
    noise = jax.random.normal(keys[3], (NBLK, NB, NB), jnp.float32)
    slow = jax.random.uniform(keys[0], (NBLK, NB), jnp.float32) < share
    fast_rate = jnp.exp(jax.random.uniform(keys[1], (NBLK, NB), jnp.float32, math.log(0.15), math.log(0.5)))
    spread = jax.random.uniform(keys[2], (NBLK, NB), jnp.float32, 0.2, 0.8)
    slow_rate = jnp.sqrt(jnp.exp(-2.0 * spread / NBLK) - 0.05)
    places = jax.random.randint(keys[4], (2,), 1, NBLK)
    block_index = jnp.arange(NBLK)
    struck = jnp.any(block_index[:, None] == places[None, :], axis=1)
    losses = jax.random.uniform(keys[5], (NBLK, 1), jnp.float32, 0.55, 0.8)
    slow_rate = jnp.where(struck[:, None], slow_rate * losses, slow_rate)
    rate = jnp.where(slow, slow_rate, fast_rate)
    return -(noise * (0.2 / math.sqrt(NB)) + rate[:, :, None] * jnp.eye(NB, dtype=jnp.float32))


def steps_of(rng, extent, pieces, least, largest):
    factor_of, own = 1.0, jax.random.fold_in(rng, 6)
    for dim, blocks in pieces:
        steps = jnp.exp(jax.random.uniform(jax.random.fold_in(own, dim), (blocks,), jnp.float32, least / len(pieces), largest / len(pieces)))
        factor_of = factor_of * jnp.repeat(steps, extent[dim] // blocks).reshape([-1 if axis == dim else 1 for axis in range(len(extent))])
    return factor_of


def bell_draw(rng, dims, scale, reach, shards=(), kind=jnp.bfloat16):
    entries = jax.random.normal(rng, dims, jnp.float32) * scale
    if len(shards) > 0:
        entries = steps_of(rng, dims, shards, -0.22, 0.18) * entries
    return jnp.clip(entries, min=-reach, max=reach).astype(kind)


def setup_inputs(seed: int = 0) -> dict:
    streams_of = jax.random.split(jax.random.key(seed), 7)
    diag_inverse = draw_diag_inverse(jax.random.fold_in(streams_of[6], 71), 0)
    coupling = draw_coupling(jax.random.fold_in(streams_of[6], 71), 0)
    rhs_t = bell_draw(streams_of[2], (RHS, N), 0.4, 2.4, ((0, 8), (1, 64)), jnp.float32)
    prior = bell_draw(streams_of[3], (RHS, NB), 1.0, 6.0, ((0, 8),), jnp.float32)
    border_factor = bell_draw(streams_of[4], (BORDER, N), N ** -0.5, 0.03125, ((0, 8), (1, 64)), jnp.float32)
    border_rhs = bell_draw(streams_of[5], (RHS, BORDER), 1.0, 6.0, ((0, 8),), jnp.float32)
    return {"diag_inverse": diag_inverse, "coupling": coupling, "rhs_t": rhs_t, "prior": prior, "border_factor": border_factor, "border_rhs": border_rhs}


def times_transposed(left_side, matrix):
    return lax.dot_general(left_side, matrix, (((1,), (1,)), ((), ())), precision=lax.Precision.HIGHEST, preferred_element_type=jnp.float32)


def reference(diag_inverse, coupling, rhs_t, prior, border_factor, border_rhs):
    blocks = rhs_t.reshape(RHS, NBLK, NB).transpose(1, 0, 2)

    def advance(previous, inputs):
        inverse, link, right_side = inputs
        coupled = times_transposed(previous, link)
        current = times_transposed(right_side - coupled, inverse)
        return current, current

    final_block, solved = lax.scan(advance, prior, (diag_inverse, coupling, blocks))
    solution = solved.transpose(1, 0, 2).reshape(RHS, NBLK * NB)
    border_out = border_rhs - times_transposed(solution, border_factor)
    return solution, border_out
```

```python
import jax
import jax.numpy as jnp
from jax import lax
from jax.sharding import PartitionSpec as P

PLANES, CHIPS, CORES = 8, 4, 2
IN_PLANE = CHIPS * CORES
BLOCK_SHIFT = 4


def device(plane, chip, core):
    return (plane * CHIPS + chip) * CORES + core


CORE_SWAP = [(p, p ^ 1) for p in range(PLANES * IN_PLANE)]
CHIP_GROUPS = [[device(z, c, k) for c in range(CHIPS)] for z in range(PLANES) for k in range(CORES)]
PLANE_GROUPS = [[device(z, c, k) for z in range(PLANES)] for c in range(CHIPS) for k in range(CORES)]


def product(left, right):
    return lax.dot_general(left, right, (((1,), (0,)), ((), ())), precision=lax.Precision.HIGH, preferred_element_type=jnp.float32)


def product_transposed(left, right):
    return lax.dot_general(left, right, (((1,), (1,)), ((), ())), precision=lax.Precision.HIGH, preferred_element_type=jnp.float32)


def to_all(value, axis, count, groups=None):
    copies = jnp.broadcast_to(value[None], (count,) + value.shape)
    return lax.all_to_all(copies, axis, 0, 0, axis_index_groups=groups)


def exchanged(pieces, axis, groups=None):
    return lax.all_to_all(pieces, axis, 0, 0, axis_index_groups=groups)


def swapped(value):
    return lax.ppermute(value, "blk", CORE_SWAP)


def after(map_and_offset, step, shift, size):
    made = product(map_and_offset, step[:size])
    return jnp.concatenate([made[:size], made[size:] * (2.0**shift) + step[size:]], axis=0)


def body(diag_inverse, coupling, rhs_t, prior, border_factor, border_rhs):
    rows, size = rhs_t.shape
    members = lax.axis_size("rhs")
    position = lax.axis_index("blk")
    core = position % CORES
    chip = (position // CORES) % CHIPS
    plane = position // IN_PLANE
    first_core = core == 0

    own = jnp.concatenate([coupling[0], diag_inverse[0]], axis=0)
    gathered = to_all(own, "rhs", members)
    share = coupling.shape[1]
    link = gathered[:, :share].reshape(size, size)
    inverse = gathered[:, share:].reshape(size, size)

    border_factor, gathered = lax.optimization_barrier((border_factor, gathered))
    border_block = lax.all_gather(border_factor, "rhs", axis=0, tiled=True)

    block_map = lax.dot_general(link, inverse, (((0,), (1,)), ((), ())), precision=lax.Precision.HIGH, preferred_element_type=jnp.float32)
    block = jnp.concatenate([block_map * (-(2.0**-BLOCK_SHIFT)), product_transposed(rhs_t, inverse)], axis=0)

    other = swapped(block)
    pair = after(jnp.where(first_core, block, other), jnp.where(first_core, other, block), BLOCK_SHIFT, size)

    half, half_rows = size // CORES, rows // CORES
    part = jnp.concatenate(
        [lax.dynamic_slice_in_dim(pair, core * half, half, 0), lax.dynamic_slice_in_dim(pair, size + core * half_rows, half_rows, 0)], axis=0
    )
    mine = to_all(part, "blk", CHIPS, CHIP_GROUPS)
    theirs = swapped(mine)
    upper, lower = jnp.where(first_core, mine, theirs), jnp.where(first_core, theirs, mine)
    chips = [jnp.concatenate([upper[c, :half], lower[c, :half], upper[c, half:], lower[c, half:]], axis=0) for c in range(CHIPS)]

    prefixes = [chips[0]]
    for c in range(1, CHIPS):
        prefixes.append(after(prefixes[-1], chips[c], 2 * BLOCK_SHIFT, size))
    whole = prefixes[-1]

    start = prior
    for step in range(1, PLANES):
        end = product(start, whole[:size]) * (2.0 ** (BLOCK_SHIFT * IN_PLANE)) + whole[size:]
        hop = [(device(step - 1, c, k), device(step, c, k)) for c in range(CHIPS) for k in range(CORES)]
        arrived = lax.ppermute(end, "blk", hop)
        start = jnp.where(plane == step, arrived, start)

    before = jnp.where(chip == 1, prefixes[0], jnp.where(chip == 2, prefixes[1], prefixes[2]))
    even = jnp.where(chip == 0, block, after(before, block, BLOCK_SHIFT, size))
    odd = jnp.where(chip == CHIPS - 1, whole, jnp.where(chip == 0, prefixes[0], jnp.where(chip == 1, prefixes[1], prefixes[2])))
    mapped = jnp.where(first_core, even, odd)
    scales = jnp.asarray([2.0 ** (BLOCK_SHIFT * (q + 1)) for q in range(IN_PLANE)], jnp.float32)
    solved = product(start, mapped[:size]) * scales[position % IN_PLANE] + mapped[size:]

    border = border_rhs.shape[1]
    partial = product_transposed(solved, border_block)
    per_core, per_chip = border // CORES, border // CORES // CHIPS
    per_plane = rows // PLANES
    kept = lax.dynamic_slice_in_dim(partial, core * per_core, per_core, 1)
    passed = lax.dynamic_slice_in_dim(partial, (1 - core) * per_core, per_core, 1)
    total = kept + swapped(passed)
    pieces = jnp.transpose(total.reshape(rows, CHIPS, per_chip), (1, 0, 2))
    total = jnp.sum(exchanged(pieces, "blk", CHIP_GROUPS), axis=0)
    total = jnp.sum(exchanged(total.reshape(PLANES, per_plane, per_chip), "blk", PLANE_GROUPS), axis=0)
    held = lax.dynamic_slice(border_rhs, (plane * per_plane, core * per_core + chip * per_chip), (per_plane, per_chip))
    result = to_all(held - total, "blk", PLANES, PLANE_GROUPS).reshape(rows, per_chip)
    result = to_all(result, "blk", CHIPS, CHIP_GROUPS)
    result = jnp.transpose(result, (1, 0, 2)).reshape(rows, per_core)
    across = swapped(result)
    left, right = jnp.where(first_core, result, across), jnp.where(first_core, across, result)
    return solved, jnp.concatenate([left, right], axis=1)


def solution(mesh):
    placed = (
        P("blk", "rhs", None),
        P("blk", "rhs", None),
        P("rhs", "blk"),
        P("rhs", None),
        P("rhs", "blk"),
        P("rhs", None),
    )
    return jax.shard_map(
        body,
        mesh=mesh,
        in_specs=placed,
        out_specs=(P("rhs", "blk"), P("rhs", None)),
        check_vma=False,
    )
```

```python
import jax
import jax.numpy as jnp
from jax import lax
from jax.sharding import PartitionSpec as P

PLANES, CHIPS, CORES = 8, 4, 2
IN_PLANE = CHIPS * CORES
BLOCK_SHIFT = 4


def device(plane, chip, core):
    return (plane * CHIPS + chip) * CORES + core


CORE_SWAP = [(p, p ^ 1) for p in range(PLANES * IN_PLANE)]
CHIP_GROUPS = [[device(z, c, k) for c in range(CHIPS)] for z in range(PLANES) for k in range(CORES)]
PLANE_GROUPS = [[device(z, c, k) for z in range(PLANES)] for c in range(CHIPS) for k in range(CORES)]


def product(left, right):
    return lax.dot_general(left, right, (((1,), (0,)), ((), ())), precision=lax.Precision.HIGH, preferred_element_type=jnp.float32)


def product_transposed(left, right):
    return lax.dot_general(left, right, (((1,), (1,)), ((), ())), precision=lax.Precision.HIGH, preferred_element_type=jnp.float32)


def to_all(value, axis, count, groups=None):
    copies = jnp.broadcast_to(value[None], (count,) + value.shape)
    return lax.all_to_all(copies, axis, 0, 0, axis_index_groups=groups)


def exchanged(pieces, axis, groups=None):
    return lax.all_to_all(pieces, axis, 0, 0, axis_index_groups=groups)


def chip_turn(count):
    return [(device(z, c, k), device(z, (c + count) % CHIPS, k)) for z in range(PLANES) for c in range(CHIPS) for k in range(CORES)]


def swapped(value):
    return lax.ppermute(value, "blk", CORE_SWAP)


def after(map_and_offset, step, shift, size):
    made = product(map_and_offset, step[:size])
    return jnp.concatenate([made[:size], made[size:] * (2.0**shift) + step[size:]], axis=0)


def body(diag_inverse, coupling, rhs_t, prior, border_factor, border_rhs):
    rows, size = rhs_t.shape
    members = lax.axis_size("rhs")
    position = lax.axis_index("blk")
    core = position % CORES
    chip = (position // CORES) % CHIPS
    plane = position // IN_PLANE
    first_core = core == 0

    own = jnp.concatenate([coupling[0], diag_inverse[0]], axis=0)
    gathered = to_all(own, "rhs", members)
    share = coupling.shape[1]
    link = gathered[:, :share].reshape(size, size)
    inverse = gathered[:, share:].reshape(size, size)

    block_map = lax.dot_general(link, inverse, (((0,), (1,)), ((), ())), precision=lax.Precision.HIGH, preferred_element_type=jnp.float32)
    block = jnp.concatenate([block_map * (-(2.0**-BLOCK_SHIFT)), product_transposed(rhs_t, inverse)], axis=0)

    other = swapped(block)
    pair = after(jnp.where(first_core, block, other), jnp.where(first_core, other, block), BLOCK_SHIFT, size)

    half, half_rows = size // CORES, rows // CORES
    part = jnp.concatenate(
        [lax.dynamic_slice_in_dim(pair, core * half, half, 0), lax.dynamic_slice_in_dim(pair, size + core * half_rows, half_rows, 0)], axis=0
    )
    mine = jnp.stack([lax.ppermute(part, "blk", chip_turn(k)) for k in range(1, CHIPS)])
    theirs = swapped(mine)
    upper, lower = jnp.where(first_core, mine, theirs), jnp.where(first_core, theirs, mine)
    fetched = jnp.concatenate([upper[:, :half], lower[:, :half], upper[:, half:], lower[:, half:]], axis=1)
    chips = jnp.concatenate([pair[None], fetched], axis=0)

    def chip_map(c):
        return lax.dynamic_index_in_dim(chips, (chip - c) % CHIPS, 0, keepdims=False)

    prefixes = [chip_map(0)]
    for c in range(1, CHIPS):
        prefixes.append(after(prefixes[-1], chip_map(c), 2 * BLOCK_SHIFT, size))
    whole = prefixes[-1]

    before = jnp.where(chip == 1, prefixes[0], jnp.where(chip == 2, prefixes[1], prefixes[2]))
    even = jnp.where(chip == 0, block, after(before, block, BLOCK_SHIFT, size))
    odd = jnp.where(chip == CHIPS - 1, whole, jnp.where(chip == 0, prefixes[0], jnp.where(chip == 1, prefixes[1], prefixes[2])))
    mapped = jnp.where(first_core, even, odd)
    scales = jnp.asarray([2.0 ** (BLOCK_SHIFT * (q + 1 - IN_PLANE)) for q in range(IN_PLANE)], jnp.float32)
    own_map = mapped[:size] * scales[position % IN_PLANE]
    own_offset = mapped[size:]

    border = border_rhs.shape[1]
    share = border_factor.shape[0]
    piece = share // IN_PLANE

    def gather_offsets(offset):
        return to_all(offset, "rhs", members).reshape(rows * members, size)

    def border_product(offsets):
        made = product_transposed(border_factor, jnp.concatenate([own_map, offsets], axis=0))
        half_share = share // CORES
        kept = lax.dynamic_slice_in_dim(made, core * half_share, half_share, 0)
        passed = lax.dynamic_slice_in_dim(made, (1 - core) * half_share, half_share, 0)
        return kept + swapped(passed)

    def sum_chips(made):
        pieces = made.reshape(CHIPS, piece, made.shape[1])
        return jnp.sum(exchanged(pieces, "blk", CHIP_GROUPS), axis=0)

    def gather_border(made):
        return to_all(made, "rhs", members).reshape(members * piece, made.shape[1])

    beside = {3: gather_offsets, 4: border_product, 6: sum_chips, 7: gather_border}

    start = prior
    side = own_offset
    for step in range(1, PLANES):
        end = product(start, whole[:size]) * (2.0 ** (BLOCK_SHIFT * IN_PLANE)) + whole[size:]
        if step in beside:
            end, side = lax.optimization_barrier((end, side))
            side = beside[step](side)
        hop = [(device(step - 1, c, k), device(step, c, k)) for c in range(CHIPS) for k in range(CORES)]
        arrived = lax.ppermute(end, "blk", hop)
        if step in beside:
            arrived, side = lax.optimization_barrier((arrived, side))
        start = jnp.where(plane == step, arrived, start)

    large = 2.0 ** (BLOCK_SHIFT * IN_PLANE)
    solved = product(start, own_map) * large + own_offset

    member = lax.axis_index("rhs")
    chosen = (jnp.arange(rows)[:, None] + member * rows == jnp.arange(rows * members)[None, :]).astype(jnp.float32)
    fixed = product_transposed(chosen, side[:, size:])
    held = border_rhs.reshape(rows, members, CORES, CHIPS, piece)
    held = lax.dynamic_slice(held, (0, 0, core, chip, 0), (rows, members, 1, 1, piece)).reshape(rows, members * piece)
    fixed = fixed - jnp.where(plane == 0, held, 0.0)
    result = product_transposed(start, side[:, :size]) * large + fixed
    result = -jnp.sum(to_all(result, "blk", PLANES, PLANE_GROUPS), axis=0)
    result = to_all(result, "blk", CHIPS, CHIP_GROUPS)
    across = swapped(result)
    left, right = jnp.where(first_core, result, across), jnp.where(first_core, across, result)
    result = jnp.stack([left, right]).reshape(CORES, CHIPS, rows, members, piece)
    return solved, jnp.transpose(result, (2, 3, 0, 1, 4)).reshape(rows, border)


def solution(mesh):
    placed = (
        P("blk", "rhs", None),
        P("blk", "rhs", None),
        P("rhs", "blk"),
        P("rhs", None),
        P("rhs", "blk"),
        P("rhs", None),
    )
    return jax.shard_map(
        body,
        mesh=mesh,
        in_specs=placed,
        out_specs=(P("rhs", "blk"), P("rhs", None)),
        check_vma=False,
    )
```

```python
import jax
import jax.numpy as jnp
from jax import lax
from jax.sharding import PartitionSpec as P

PLANES, CHIPS, CORES = 8, 4, 2
BLOCKS = PLANES * CHIPS * CORES
SHIFT = 4


def device(plane, chip, core):
    return (plane * CHIPS + chip) * CORES + core


CORE_SWAP = [(p, p ^ 1) for p in range(BLOCKS)]
TO_EVEN = [(p + 1, p) for p in range(0, BLOCKS, CORES)]
NEXT_CHIP = [(p, p + CORES) for p in range(BLOCKS - CORES)]
CORE_GROUPS = [[device(z, c, k) for z in range(PLANES) for c in range(CHIPS)] for k in range(CORES)]


def product(left, right):
    return lax.dot_general(left, right, (((1,), (0,)), ((), ())), precision=lax.Precision.HIGH, preferred_element_type=jnp.float32)


def product_transposed(left, right):
    return lax.dot_general(left, right, (((1,), (1,)), ((), ())), precision=lax.Precision.HIGH, preferred_element_type=jnp.float32)


def exchanged(pieces, axis, groups=None):
    return lax.all_to_all(pieces, axis, 0, 0, axis_index_groups=groups)


def to_all(value, axis, count, groups=None):
    return exchanged(jnp.broadcast_to(value[None], (count,) + value.shape), axis, groups)


def permuted(value, pairs):
    return lax.ppermute(value, "blk", pairs)


def body(diag_inverse, coupling, rhs_t, prior, border_factor, border_rhs):
    rows, size = rhs_t.shape
    members = lax.axis_size("rhs")
    member = lax.axis_index("rhs")
    position = lax.axis_index("blk")
    core = position % CORES
    chip = (position // CORES) % CHIPS
    plane = position // (CORES * CHIPS)
    even = core == 0

    share = coupling.shape[1]
    gathered = to_all(jnp.concatenate([coupling[0], diag_inverse[0]], axis=0), "rhs", members)
    link = gathered[:, :share].reshape(size, size)
    inverse = gathered[:, share:].reshape(size, size)

    block_map = lax.dot_general(link, inverse, (((0,), (1,)), ((), ())), precision=lax.Precision.HIGH, preferred_element_type=jnp.float32)
    block_map = block_map * (-(2.0**-SHIFT))
    offset = product_transposed(rhs_t, inverse)
    offset = jnp.where(position == 0, offset + product(prior, block_map) * 2.0**SHIFT, offset)

    block = jnp.concatenate([block_map, offset], axis=0)
    other = permuted(block, CORE_SWAP)
    first, second = jnp.where(even, block, other), jnp.where(even, other, block)
    pair = product(first, second[:size])
    chip_map = pair[:size]
    chip_offset = pair[size:] * 2.0**SHIFT + second[size:]

    state = jnp.where(even, lax.dynamic_slice_in_dim(chip_map, member * rows, rows, 0), chip_offset)
    factor = jnp.where(even, 1.0, 2.0 ** (2 * SHIFT))
    added = jnp.where(even, 0.0, chip_offset)
    for _ in range(CHIPS - 2):
        state = product(permuted(state, NEXT_CHIP), chip_map) * factor + added
    state = permuted(state, NEXT_CHIP)
    across = permuted(state, CORE_SWAP)
    window = jnp.concatenate([jnp.where(even, state, across), jnp.where(even, across, state)], axis=0)
    window = product(window, jnp.where(even, block_map, chip_map))
    own_offset = window[rows:] * jnp.where(even, 2.0**SHIFT, 2.0 ** (2 * SHIFT)) + jnp.where(even, offset, chip_offset)
    scale = jnp.where(even, 2.0 ** (SHIFT * (2 * CHIPS - 1)), 2.0 ** (SHIFT * 2 * CHIPS))

    arrived = permuted(own_offset, [(device(0, c, 1), device(1, c, 1)) for c in range(CHIPS)])
    own_map = to_all(window[:rows], "rhs", members).reshape(size, size)
    start = jnp.where(plane == 1, arrived, 0.0)
    border_block = None
    for step in range(2, PLANES):
        end = product(start, own_map) * scale + own_offset
        if step == 3:
            end, border_factor = lax.optimization_barrier((end, border_factor))
            border_block = to_all(border_factor, "rhs", members)
        arrived = permuted(end, [(device(step - 1, c, 1), device(step, c, 1)) for c in range(CHIPS)])
        start = jnp.where(plane == step, arrived, start)
    start = jnp.where(even, permuted(start, TO_EVEN), start)
    solved = product(start, own_map) * scale + own_offset

    border = border_rhs.shape[1]
    border_block = border_block.reshape(border, size)
    partial = product_transposed(solved, border_block)
    per_core, per_chip = border // CORES, border // CORES // CHIPS
    per_plane = rows // PLANES
    kept = lax.dynamic_slice_in_dim(partial, core * per_core, per_core, 1)
    passed = lax.dynamic_slice_in_dim(partial, (1 - core) * per_core, per_core, 1)
    total = kept + permuted(passed, CORE_SWAP)
    pieces = jnp.transpose(total.reshape(PLANES, per_plane, CHIPS, per_chip), (0, 2, 1, 3))
    pieces = pieces.reshape(PLANES * CHIPS, per_plane, per_chip)
    total = jnp.sum(exchanged(pieces, "blk", CORE_GROUPS), axis=0)
    held = lax.dynamic_slice(border_rhs, (plane * per_plane, core * per_core + chip * per_chip), (per_plane, per_chip))
    result = to_all(held - total, "blk", PLANES * CHIPS, CORE_GROUPS)
    result = result.reshape(PLANES, CHIPS, per_plane, per_chip)
    result = jnp.transpose(result, (0, 2, 1, 3)).reshape(rows, per_core)
    across = permuted(result, CORE_SWAP)
    return solved, jnp.concatenate([jnp.where(even, result, across), jnp.where(even, across, result)], axis=1)


def solution(mesh):
    placed = (
        P("blk", "rhs", None),
        P("blk", "rhs", None),
        P("rhs", "blk"),
        P("rhs", None),
        P("rhs", "blk"),
        P("rhs", None),
    )
    return jax.shard_map(
        body,
        mesh=mesh,
        in_specs=placed,
        out_specs=(P("rhs", "blk"), P("rhs", None)),
        check_vma=False,
    )
```

```python
import jax
import jax.numpy as jnp
from jax import lax
from jax.sharding import PartitionSpec as P

PLANES, CHIPS, CORES = 8, 4, 2
BLOCKS = PLANES * CHIPS * CORES
SHIFT = 4


def device(plane, chip, core):
    return (plane * CHIPS + chip) * CORES + core


CORE_SWAP = [(p, p ^ 1) for p in range(BLOCKS)]
TO_EVEN = [(p + 1, p) for p in range(0, BLOCKS, CORES)]
NEXT_CHIP = [(p, p + CORES) for p in range(BLOCKS - CORES)]
CORE_GROUPS = [[device(z, c, k) for z in range(PLANES) for c in range(CHIPS)] for k in range(CORES)]


def product(left, right):
    return lax.dot_general(left, right, (((1,), (0,)), ((), ())), precision=lax.Precision.HIGH, preferred_element_type=jnp.float32)


def product_transposed(left, right):
    return lax.dot_general(left, right, (((1,), (1,)), ((), ())), precision=lax.Precision.HIGH, preferred_element_type=jnp.float32)


def exchanged(pieces, axis, groups=None):
    return lax.all_to_all(pieces, axis, 0, 0, axis_index_groups=groups)


def to_all(value, axis, count, groups=None):
    return exchanged(jnp.broadcast_to(value[None], (count,) + value.shape), axis, groups)


def permuted(value, pairs):
    return lax.ppermute(value, "blk", pairs)


def body(diag_inverse, coupling, rhs_t, prior, border_factor, border_rhs):
    rows, size = rhs_t.shape
    members = lax.axis_size("rhs")
    member = lax.axis_index("rhs")
    position = lax.axis_index("blk")
    core = position % CORES
    chip = (position // CORES) % CHIPS
    plane = position // (CORES * CHIPS)
    even = core == 0

    share = coupling.shape[1]
    gathered = to_all(jnp.concatenate([coupling[0], diag_inverse[0]], axis=0), "rhs", members)
    link = gathered[:, :share].reshape(size, size)
    inverse = gathered[:, share:].reshape(size, size)

    block_map = lax.dot_general(link, inverse, (((0,), (1,)), ((), ())), precision=lax.Precision.HIGH, preferred_element_type=jnp.float32)
    block_map = block_map * (-(2.0**-SHIFT))
    offset = product_transposed(rhs_t, inverse)
    offset = jnp.where(position == 0, offset + product(prior, block_map) * 2.0**SHIFT, offset)

    block = jnp.concatenate([block_map, offset], axis=0)
    other = permuted(block, CORE_SWAP)
    first, second = jnp.where(even, block, other), jnp.where(even, other, block)
    pair = product(first, second[:size])
    chip_map = pair[:size]
    chip_offset = pair[size:] * 2.0**SHIFT + second[size:]

    state = jnp.where(even, lax.dynamic_slice_in_dim(chip_map, member * rows, rows, 0), chip_offset)
    factor = jnp.where(even, 1.0, 2.0 ** (2 * SHIFT))
    added = jnp.where(even, 0.0, chip_offset)
    for _ in range(CHIPS - 2):
        state = product(permuted(state, NEXT_CHIP), chip_map) * factor + added
    state = permuted(state, NEXT_CHIP)
    across = permuted(state, CORE_SWAP)
    window = jnp.concatenate([jnp.where(even, state, across), jnp.where(even, across, state)], axis=0)
    window = product(window, jnp.where(even, block_map, chip_map))
    own_offset = window[rows:] * jnp.where(even, 2.0**SHIFT, 2.0 ** (2 * SHIFT)) + jnp.where(even, offset, chip_offset)
    scale = jnp.where(even, 2.0 ** (SHIFT * (2 * CHIPS - 1)), 2.0 ** (SHIFT * 2 * CHIPS))

    arrived = permuted(own_offset, [(device(0, c, 1), device(1, c, 1)) for c in range(CHIPS)])
    own_map = to_all(window[:rows], "rhs", members).reshape(size, size)
    copies = jnp.broadcast_to(border_factor[None], (members,) + border_factor.shape)
    arrived, copies = lax.optimization_barrier((arrived, copies))
    border_block = exchanged(copies, "rhs")
    start = jnp.where(plane == 1, arrived, 0.0)
    for step in range(2, PLANES):
        end = product(start, own_map) * scale + own_offset
        arrived = permuted(end, [(device(step - 1, c, 1), device(step, c, 1)) for c in range(CHIPS)])
        start = jnp.where(plane == step, arrived, start)
    start = jnp.where(even, permuted(start, TO_EVEN), start)
    solved = product(start, own_map) * scale + own_offset

    border = border_rhs.shape[1]
    border_block = border_block.reshape(border, size)
    partial = product_transposed(solved, border_block)
    per_core, per_chip = border // CORES, border // CORES // CHIPS
    per_plane = rows // PLANES
    kept = lax.dynamic_slice_in_dim(partial, core * per_core, per_core, 1)
    passed = lax.dynamic_slice_in_dim(partial, (1 - core) * per_core, per_core, 1)
    total = kept + permuted(passed, CORE_SWAP)
    pieces = jnp.transpose(total.reshape(PLANES, per_plane, CHIPS, per_chip), (0, 2, 1, 3))
    pieces = pieces.reshape(PLANES * CHIPS, per_plane, per_chip)
    total = jnp.sum(exchanged(pieces, "blk", CORE_GROUPS), axis=0)
    held = lax.dynamic_slice(border_rhs, (plane * per_plane, core * per_core + chip * per_chip), (per_plane, per_chip))
    result = to_all(held - total, "blk", PLANES * CHIPS, CORE_GROUPS)
    result = result.reshape(PLANES, CHIPS, per_plane, per_chip)
    result = jnp.transpose(result, (0, 2, 1, 3)).reshape(rows, per_core)
    across = permuted(result, CORE_SWAP)
    return solved, jnp.concatenate([jnp.where(even, result, across), jnp.where(even, across, result)], axis=1)


def solution(mesh):
    placed = (
        P("blk", "rhs", None),
        P("blk", "rhs", None),
        P("rhs", "blk"),
        P("rhs", None),
        P("rhs", "blk"),
        P("rhs", None),
    )
    return jax.shard_map(
        body,
        mesh=mesh,
        in_specs=placed,
        out_specs=(P("rhs", "blk"), P("rhs", None)),
        check_vma=False,
    )
```

```python
import jax
import jax.numpy as jnp
from jax import lax
from jax.sharding import PartitionSpec as P

PLANES, CHIPS, CORES = 8, 4, 2
BLOCKS = PLANES * CHIPS * CORES
SHIFT = 4


def device(plane, chip, core):
    return (plane * CHIPS + chip) * CORES + core


CORE_SWAP = [(p, p ^ 1) for p in range(BLOCKS)]
TO_EVEN = [(p + 1, p) for p in range(0, BLOCKS, CORES)]
NEXT_CHIP = [(p, p + CORES) for p in range(BLOCKS - CORES)]
CORE_GROUPS = [[device(z, c, k) for z in range(PLANES) for c in range(CHIPS)] for k in range(CORES)]


def product(left, right):
    return lax.dot_general(left, right, (((1,), (0,)), ((), ())), precision=lax.Precision.HIGH, preferred_element_type=jnp.float32)


def product_transposed(left, right):
    return lax.dot_general(left, right, (((1,), (1,)), ((), ())), precision=lax.Precision.HIGH, preferred_element_type=jnp.float32)


def exchanged(pieces, axis, groups=None):
    return lax.all_to_all(pieces, axis, 0, 0, axis_index_groups=groups)


def to_all(value, axis, count, groups=None):
    return exchanged(jnp.broadcast_to(value[None], (count,) + value.shape), axis, groups)


def permuted(value, pairs):
    return lax.ppermute(value, "blk", pairs)


def body(diag_inverse, coupling, rhs_t, prior, border_factor, border_rhs):
    rows, size = rhs_t.shape
    members = lax.axis_size("rhs")
    member = lax.axis_index("rhs")
    position = lax.axis_index("blk")
    core = position % CORES
    chip = (position // CORES) % CHIPS
    plane = position // (CORES * CHIPS)
    even = core == 0

    share = coupling.shape[1]
    gathered = to_all(jnp.concatenate([coupling[0], diag_inverse[0]], axis=0), "rhs", members)
    link = gathered[:, :share].reshape(size, size)
    inverse = gathered[:, share:].reshape(size, size)

    block_map = lax.dot_general(link, inverse, (((0,), (1,)), ((), ())), precision=lax.Precision.HIGH, preferred_element_type=jnp.float32)
    block_map = block_map * (-(2.0**-SHIFT))
    offset = product_transposed(rhs_t, inverse)
    offset = jnp.where(position == 0, offset + product(prior, block_map) * 2.0**SHIFT, offset)

    block = jnp.concatenate([block_map, offset], axis=0)
    other = permuted(block, CORE_SWAP)
    border = border_rhs.shape[1]
    half = size // 2

    def border_copies(part):
        return jnp.broadcast_to(part[None], (members,) + part.shape)

    other, copies = lax.optimization_barrier((other, border_copies(border_factor[:, :half])))
    border_left = exchanged(copies, "rhs")

    first, second = jnp.where(even, block, other), jnp.where(even, other, block)
    pair = product(first, second[:size])
    chip_map = pair[:size]
    chip_offset = pair[size:] * 2.0**SHIFT + second[size:]

    state = jnp.where(even, lax.dynamic_slice_in_dim(chip_map, member * rows, rows, 0), chip_offset)
    factor = jnp.where(even, 1.0, 2.0 ** (2 * SHIFT))
    added = jnp.where(even, 0.0, chip_offset)
    for _ in range(CHIPS - 2):
        state = product(permuted(state, NEXT_CHIP), chip_map) * factor + added
    state = permuted(state, NEXT_CHIP)
    across = permuted(state, CORE_SWAP)
    window = jnp.concatenate([jnp.where(even, state, across), jnp.where(even, across, state)], axis=0)
    window = product(window, jnp.where(even, block_map, chip_map))
    own_offset = window[rows:] * jnp.where(even, 2.0**SHIFT, 2.0 ** (2 * SHIFT)) + jnp.where(even, offset, chip_offset)
    scale = jnp.where(even, 2.0 ** (SHIFT * (2 * CHIPS - 1)), 2.0 ** (SHIFT * 2 * CHIPS))

    arrived = permuted(own_offset, [(device(0, c, 1), device(1, c, 1)) for c in range(CHIPS)])
    own_map = to_all(window[:rows], "rhs", members).reshape(size, size)
    arrived, copies = lax.optimization_barrier((arrived, border_copies(border_factor[:, half:])))
    border_right = exchanged(copies, "rhs")
    start = jnp.where(plane == 1, arrived, 0.0)
    for step in range(2, PLANES):
        end = product(start, own_map) * scale + own_offset
        arrived = permuted(end, [(device(step - 1, c, 1), device(step, c, 1)) for c in range(CHIPS)])
        start = jnp.where(plane == step, arrived, start)
    start = jnp.where(even, permuted(start, TO_EVEN), start)
    solved = product(start, own_map) * scale + own_offset

    partial = product_transposed(solved[:, :half], border_left.reshape(border, half))
    partial = partial + product_transposed(solved[:, half:], border_right.reshape(border, half))
    per_core, per_chip = border // CORES, border // CORES // CHIPS
    per_plane = rows // PLANES
    kept = lax.dynamic_slice_in_dim(partial, core * per_core, per_core, 1)
    passed = lax.dynamic_slice_in_dim(partial, (1 - core) * per_core, per_core, 1)
    total = kept + permuted(passed, CORE_SWAP)
    pieces = jnp.transpose(total.reshape(PLANES, per_plane, CHIPS, per_chip), (0, 2, 1, 3))
    pieces = pieces.reshape(PLANES * CHIPS, per_plane, per_chip)
    total = jnp.sum(exchanged(pieces, "blk", CORE_GROUPS), axis=0)
    held = lax.dynamic_slice(border_rhs, (plane * per_plane, core * per_core + chip * per_chip), (per_plane, per_chip))
    result = to_all(held - total, "blk", PLANES * CHIPS, CORE_GROUPS)
    result = result.reshape(PLANES, CHIPS, per_plane, per_chip)
    result = jnp.transpose(result, (0, 2, 1, 3)).reshape(rows, per_core)
    across = permuted(result, CORE_SWAP)
    return solved, jnp.concatenate([jnp.where(even, result, across), jnp.where(even, across, result)], axis=1)


def solution(mesh):
    placed = (
        P("blk", "rhs", None),
        P("blk", "rhs", None),
        P("rhs", "blk"),
        P("rhs", None),
        P("rhs", "blk"),
        P("rhs", None),
    )
    return jax.shard_map(
        body,
        mesh=mesh,
        in_specs=placed,
        out_specs=(P("rhs", "blk"), P("rhs", None)),
        check_vma=False,
    )
```

```python
import jax
import jax.numpy as jnp
from jax import lax
from jax.sharding import PartitionSpec as P

PLANES, CHIPS, CORES = 8, 4, 2
BLOCKS = PLANES * CHIPS * CORES
SHIFT = 4


def device(plane, chip, core):
    return (plane * CHIPS + chip) * CORES + core


CORE_SWAP = [(p, p ^ 1) for p in range(BLOCKS)]
TO_EVEN = [(p + 1, p) for p in range(0, BLOCKS, CORES)]
NEXT_CHIP = [(p, p + CORES) for p in range(BLOCKS - CORES)]
CORE_GROUPS = [[device(z, c, k) for z in range(PLANES) for c in range(CHIPS)] for k in range(CORES)]


def product(left, right):
    return lax.dot_general(left, right, (((1,), (0,)), ((), ())), precision=lax.Precision.HIGH, preferred_element_type=jnp.float32)


def product_transposed(left, right):
    return lax.dot_general(left, right, (((1,), (1,)), ((), ())), precision=lax.Precision.HIGH, preferred_element_type=jnp.float32)


def exchanged(pieces, axis, groups=None):
    return lax.all_to_all(pieces, axis, 0, 0, axis_index_groups=groups)


def to_all(value, axis, count, groups=None):
    return exchanged(jnp.broadcast_to(value[None], (count,) + value.shape), axis, groups)


def permuted(value, pairs):
    return lax.ppermute(value, "blk", pairs)


def body(diag_inverse, coupling, rhs_t, prior, border_factor, border_rhs):
    rows, size = rhs_t.shape
    members = lax.axis_size("rhs")
    member = lax.axis_index("rhs")
    position = lax.axis_index("blk")
    core = position % CORES
    chip = (position // CORES) % CHIPS
    plane = position // (CORES * CHIPS)
    even = core == 0

    share = coupling.shape[1]
    gathered = to_all(jnp.concatenate([coupling[0], diag_inverse[0]], axis=0), "rhs", members)
    link = gathered[:, :share].reshape(size, size)
    inverse = gathered[:, share:].reshape(size, size)

    block_map = lax.dot_general(link, inverse, (((0,), (1,)), ((), ())), precision=lax.Precision.HIGH, preferred_element_type=jnp.float32)
    block_map = block_map * (-(2.0**-SHIFT))
    offset = product_transposed(rhs_t, inverse)
    offset = jnp.where(position == 0, offset + product(prior, block_map) * 2.0**SHIFT, offset)

    block = jnp.concatenate([block_map, offset], axis=0)
    other = permuted(block, CORE_SWAP)
    border = border_rhs.shape[1]
    half = size // 2

    def border_copies(part):
        return jnp.broadcast_to(part[None], (members,) + part.shape)

    other, copies = lax.optimization_barrier((other, border_copies(border_factor[:, :half])))
    border_left = exchanged(copies, "rhs")

    first, second = jnp.where(even, block, other), jnp.where(even, other, block)
    pair = product(first, second[:size])
    chip_map = pair[:size]
    chip_offset = pair[size:] * 2.0**SHIFT + second[size:]

    state = jnp.where(even, lax.dynamic_slice_in_dim(chip_map, member * rows, rows, 0), chip_offset)
    factor = jnp.where(even, 1.0, 2.0 ** (2 * SHIFT))
    added = jnp.where(even, 0.0, chip_offset)
    for _ in range(CHIPS - 2):
        state = product(permuted(state, NEXT_CHIP), chip_map) * factor + added
    state, border_left = lax.optimization_barrier((permuted(state, NEXT_CHIP), border_left))
    across = permuted(state, CORE_SWAP)
    window = jnp.concatenate([jnp.where(even, state, across), jnp.where(even, across, state)], axis=0)
    window = product(window, jnp.where(even, block_map, chip_map))
    own_offset = window[rows:] * jnp.where(even, 2.0**SHIFT, 2.0 ** (2 * SHIFT)) + jnp.where(even, offset, chip_offset)
    scale = jnp.where(even, 2.0 ** (SHIFT * (2 * CHIPS - 1)), 2.0 ** (SHIFT * 2 * CHIPS))

    arrived = permuted(own_offset, [(device(0, c, 1), device(1, c, 1)) for c in range(CHIPS)])
    own_map = to_all(window[:rows], "rhs", members).reshape(size, size)
    arrived, copies = lax.optimization_barrier((arrived, border_copies(border_factor[:, half:])))
    border_right = exchanged(copies, "rhs")
    start = jnp.where(plane == 1, arrived, 0.0)
    for step in range(2, PLANES):
        end = product(start, own_map) * scale + own_offset
        arrived = permuted(end, [(device(step - 1, c, 1), device(step, c, 1)) for c in range(CHIPS)])
        start = jnp.where(plane == step, arrived, start)
    start = jnp.where(even, permuted(start, TO_EVEN), start)
    solved = product(start, own_map) * scale + own_offset

    partial = product_transposed(solved[:, :half], border_left.reshape(border, half))
    partial = partial + product_transposed(solved[:, half:], border_right.reshape(border, half))
    per_core, per_chip = border // CORES, border // CORES // CHIPS
    per_plane = rows // PLANES
    kept = lax.dynamic_slice_in_dim(partial, core * per_core, per_core, 1)
    passed = lax.dynamic_slice_in_dim(partial, (1 - core) * per_core, per_core, 1)
    total = kept + permuted(passed, CORE_SWAP)
    pieces = jnp.transpose(total.reshape(PLANES, per_plane, CHIPS, per_chip), (0, 2, 1, 3))
    pieces = pieces.reshape(PLANES * CHIPS, per_plane, per_chip)
    total = jnp.sum(exchanged(pieces, "blk", CORE_GROUPS), axis=0)
    held = lax.dynamic_slice(border_rhs, (plane * per_plane, core * per_core + chip * per_chip), (per_plane, per_chip))
    result = to_all(held - total, "blk", PLANES * CHIPS, CORE_GROUPS)
    result = result.reshape(PLANES, CHIPS, per_plane, per_chip)
    result = jnp.transpose(result, (0, 2, 1, 3)).reshape(rows, per_core)
    across = permuted(result, CORE_SWAP)
    return solved, jnp.concatenate([jnp.where(even, result, across), jnp.where(even, across, result)], axis=1)


def solution(mesh):
    placed = (
        P("blk", "rhs", None),
        P("blk", "rhs", None),
        P("rhs", "blk"),
        P("rhs", None),
        P("rhs", "blk"),
        P("rhs", None),
    )
    return jax.shard_map(
        body,
        mesh=mesh,
        in_specs=placed,
        out_specs=(P("rhs", "blk"), P("rhs", None)),
        check_vma=False,
    )
```

```python
import jax
import jax.numpy as jnp
from jax import lax
from jax.sharding import PartitionSpec as P

PLANES, CHIPS, CORES = 8, 4, 2
BLOCKS = PLANES * CHIPS * CORES
SHIFT = 4


def device(plane, chip, core):
    return (plane * CHIPS + chip) * CORES + core


CORE_SWAP = [(p, p ^ 1) for p in range(BLOCKS)]
TO_EVEN = [(p + 1, p) for p in range(0, BLOCKS, CORES)]
NEXT_CHIP = [(p, p + CORES) for p in range(BLOCKS - CORES)]
CORE_GROUPS = [[device(z, c, k) for z in range(PLANES) for c in range(CHIPS)] for k in range(CORES)]

ROW = 4
ROW_GROUPS = [[0, 1, 2, 3], [4, 5, 6, 7]]
ROW_SWAP = [(j, j ^ ROW) for j in range(2 * ROW)]


def product(left, right):
    return lax.dot_general(left, right, (((1,), (0,)), ((), ())), precision=lax.Precision.HIGH, preferred_element_type=jnp.float32)


def product_transposed(left, right):
    return lax.dot_general(left, right, (((1,), (1,)), ((), ())), precision=lax.Precision.HIGH, preferred_element_type=jnp.float32)


def exchanged(pieces, axis, groups=None):
    return lax.all_to_all(pieces, axis, 0, 0, axis_index_groups=groups)


def to_all(value, axis, count, groups=None):
    return exchanged(jnp.broadcast_to(value[None], (count,) + value.shape), axis, groups)


def permuted(value, pairs):
    return lax.ppermute(value, "blk", pairs)


def body(diag_inverse, coupling, rhs_t, prior, border_factor, border_rhs):
    rows, size = rhs_t.shape
    members = lax.axis_size("rhs")
    member = lax.axis_index("rhs")
    position = lax.axis_index("blk")
    core = position % CORES
    chip = (position // CORES) % CHIPS
    plane = position // (CORES * CHIPS)
    even = core == 0

    share = coupling.shape[1]
    gathered = to_all(jnp.concatenate([coupling[0], diag_inverse[0]], axis=0), "rhs", members)
    link = gathered[:, :share].reshape(size, size)
    inverse = gathered[:, share:].reshape(size, size)

    block_map = lax.dot_general(link, inverse, (((0,), (1,)), ((), ())), precision=lax.Precision.HIGH, preferred_element_type=jnp.float32)
    block_map = block_map * (-(2.0**-SHIFT))
    offset = product_transposed(rhs_t, inverse)
    offset = jnp.where(position == 0, offset + product(prior, block_map) * 2.0**SHIFT, offset)

    block = jnp.concatenate([block_map, offset], axis=0)
    other = permuted(block, CORE_SWAP)
    copies = jnp.broadcast_to(border_factor[None], (ROW,) + border_factor.shape)
    other, copies = lax.optimization_barrier((other, copies))
    border_near = exchanged(copies, "rhs", ROW_GROUPS)

    first, second = jnp.where(even, block, other), jnp.where(even, other, block)
    pair = product(first, second[:size])
    chip_map = pair[:size]
    chip_offset = pair[size:] * 2.0**SHIFT + second[size:]

    state = jnp.where(even, lax.dynamic_slice_in_dim(chip_map, member * rows, rows, 0), chip_offset)
    factor = jnp.where(even, 1.0, 2.0 ** (2 * SHIFT))
    added = jnp.where(even, 0.0, chip_offset)
    for _ in range(CHIPS - 2):
        state = product(permuted(state, NEXT_CHIP), chip_map) * factor + added
    state, border_near = lax.optimization_barrier((permuted(state, NEXT_CHIP), border_near))
    across = permuted(state, CORE_SWAP)
    window = jnp.concatenate([jnp.where(even, state, across), jnp.where(even, across, state)], axis=0)
    window = product(window, jnp.where(even, block_map, chip_map))
    own_offset = window[rows:] * jnp.where(even, 2.0**SHIFT, 2.0 ** (2 * SHIFT)) + jnp.where(even, offset, chip_offset)
    scale = jnp.where(even, 2.0 ** (SHIFT * (2 * CHIPS - 1)), 2.0 ** (SHIFT * 2 * CHIPS))

    arrived = permuted(own_offset, [(device(0, c, 1), device(1, c, 1)) for c in range(CHIPS)])
    own_map = to_all(window[:rows], "rhs", members).reshape(size, size)
    own_map, border_near = lax.optimization_barrier((own_map, border_near))
    border_far = lax.ppermute(border_near, "rhs", ROW_SWAP)
    start = jnp.where(plane == 1, arrived, 0.0)
    for step in range(2, PLANES):
        end = product(start, own_map) * scale + own_offset
        arrived = permuted(end, [(device(step - 1, c, 1), device(step, c, 1)) for c in range(CHIPS)])
        start = jnp.where(plane == step, arrived, start)
    start = jnp.where(even, permuted(start, TO_EVEN), start)
    solved = product(start, own_map) * scale + own_offset

    border = border_rhs.shape[1]
    per_core, per_chip = border // CORES, border // CORES // CHIPS
    per_plane = rows // PLANES
    near = product_transposed(solved, border_near.reshape(per_core, size))
    far = product_transposed(solved, border_far.reshape(per_core, size))
    mine = core == member // ROW
    total = jnp.where(mine, near, far) + permuted(jnp.where(mine, far, near), CORE_SWAP)
    pieces = jnp.transpose(total.reshape(PLANES, per_plane, CHIPS, per_chip), (0, 2, 1, 3))
    pieces = pieces.reshape(PLANES * CHIPS, per_plane, per_chip)
    total = jnp.sum(exchanged(pieces, "blk", CORE_GROUPS), axis=0)
    held = lax.dynamic_slice(border_rhs, (plane * per_plane, core * per_core + chip * per_chip), (per_plane, per_chip))
    result = to_all(held - total, "blk", PLANES * CHIPS, CORE_GROUPS)
    result = result.reshape(PLANES, CHIPS, per_plane, per_chip)
    result = jnp.transpose(result, (0, 2, 1, 3)).reshape(rows, per_core)
    across = permuted(result, CORE_SWAP)
    return solved, jnp.concatenate([jnp.where(even, result, across), jnp.where(even, across, result)], axis=1)


def solution(mesh):
    placed = (
        P("blk", "rhs", None),
        P("blk", "rhs", None),
        P("rhs", "blk"),
        P("rhs", None),
        P("rhs", "blk"),
        P("rhs", None),
    )
    return jax.shard_map(
        body,
        mesh=mesh,
        in_specs=placed,
        out_specs=(P("rhs", "blk"), P("rhs", None)),
        check_vma=False,
    )
```

```python
import jax
import jax.numpy as jnp
from jax import lax
from jax.sharding import PartitionSpec as P

PLANES, CHIPS, CORES = 8, 4, 2
BLOCKS = PLANES * CHIPS * CORES
SHIFT = 4


def device(plane, chip, core):
    return (plane * CHIPS + chip) * CORES + core


CORE_SWAP = [(p, p ^ 1) for p in range(BLOCKS)]
TO_EVEN = [(p + 1, p) for p in range(0, BLOCKS, CORES)]
NEXT_CHIP = [(p, p + CORES) for p in range(BLOCKS - CORES)]
CORE_GROUPS = [[device(z, c, k) for z in range(PLANES) for c in range(CHIPS)] for k in range(CORES)]

ROW = 4
ROW_GROUPS = [[0, 1, 2, 3], [4, 5, 6, 7]]
ROW_SWAP = [(j, j ^ ROW) for j in range(2 * ROW)]


def product(left, right):
    return lax.dot_general(left, right, (((1,), (0,)), ((), ())), precision=lax.Precision.HIGH, preferred_element_type=jnp.float32)


def product_transposed(left, right):
    return lax.dot_general(left, right, (((1,), (1,)), ((), ())), precision=lax.Precision.HIGH, preferred_element_type=jnp.float32)


def exchanged(pieces, axis, groups=None):
    return lax.all_to_all(pieces, axis, 0, 0, axis_index_groups=groups)


def to_all(value, axis, count, groups=None):
    return exchanged(jnp.broadcast_to(value[None], (count,) + value.shape), axis, groups)


def permuted(value, pairs):
    return lax.ppermute(value, "blk", pairs)


def body(diag_inverse, coupling, rhs_t, prior, border_factor, border_rhs):
    rows, size = rhs_t.shape
    members = lax.axis_size("rhs")
    member = lax.axis_index("rhs")
    position = lax.axis_index("blk")
    core = position % CORES
    chip = (position // CORES) % CHIPS
    plane = position // (CORES * CHIPS)
    even = core == 0

    border_across = lax.ppermute(border_factor, "rhs", ROW_SWAP)

    share = coupling.shape[1]
    gathered = to_all(jnp.concatenate([coupling[0], diag_inverse[0]], axis=0), "rhs", members)
    gathered, border_across = lax.optimization_barrier((gathered, border_across))
    link = gathered[:, :share].reshape(size, size)
    inverse = gathered[:, share:].reshape(size, size)

    block_map = lax.dot_general(link, inverse, (((0,), (1,)), ((), ())), precision=lax.Precision.HIGH, preferred_element_type=jnp.float32)
    block_map = block_map * (-(2.0**-SHIFT))
    offset = product_transposed(rhs_t, inverse)
    offset = jnp.where(position == 0, offset + product(prior, block_map) * 2.0**SHIFT, offset)

    block = jnp.concatenate([block_map, offset], axis=0)
    other = permuted(block, CORE_SWAP)
    copies = jnp.broadcast_to(border_factor[None], (ROW,) + border_factor.shape)
    other, copies = lax.optimization_barrier((other, copies))
    border_near = exchanged(copies, "rhs", ROW_GROUPS)

    first, second = jnp.where(even, block, other), jnp.where(even, other, block)
    pair = product(first, second[:size])
    chip_map = pair[:size]
    chip_offset = pair[size:] * 2.0**SHIFT + second[size:]

    state = jnp.where(even, lax.dynamic_slice_in_dim(chip_map, member * rows, rows, 0), chip_offset)
    factor = jnp.where(even, 1.0, 2.0 ** (2 * SHIFT))
    added = jnp.where(even, 0.0, chip_offset)
    for _ in range(CHIPS - 2):
        state = product(permuted(state, NEXT_CHIP), chip_map) * factor + added
    state, border_near = lax.optimization_barrier((permuted(state, NEXT_CHIP), border_near))
    across = permuted(state, CORE_SWAP)
    window = jnp.concatenate([jnp.where(even, state, across), jnp.where(even, across, state)], axis=0)
    window = product(window, jnp.where(even, block_map, chip_map))
    own_offset = window[rows:] * jnp.where(even, 2.0**SHIFT, 2.0 ** (2 * SHIFT)) + jnp.where(even, offset, chip_offset)
    scale = jnp.where(even, 2.0 ** (SHIFT * (2 * CHIPS - 1)), 2.0 ** (SHIFT * 2 * CHIPS))

    arrived = permuted(own_offset, [(device(0, c, 1), device(1, c, 1)) for c in range(CHIPS)])
    own_map = to_all(window[:rows], "rhs", members).reshape(size, size)
    own_map, copies = lax.optimization_barrier((own_map, jnp.broadcast_to(border_across[None], (ROW,) + border_across.shape)))
    border_far = exchanged(copies, "rhs", ROW_GROUPS)
    start = jnp.where(plane == 1, arrived, 0.0)
    for step in range(2, PLANES):
        end = product(start, own_map) * scale + own_offset
        arrived = permuted(end, [(device(step - 1, c, 1), device(step, c, 1)) for c in range(CHIPS)])
        if step == PLANES - 1:
            arrived, border_far = lax.optimization_barrier((arrived, border_far))
        start = jnp.where(plane == step, arrived, start)
    start = jnp.where(even, permuted(start, TO_EVEN), start)
    solved = product(start, own_map) * scale + own_offset

    border = border_rhs.shape[1]
    per_core, per_chip = border // CORES, border // CORES // CHIPS
    per_plane = rows // PLANES
    near = product_transposed(solved, border_near.reshape(per_core, size))
    far = product_transposed(solved, border_far.reshape(per_core, size))
    mine = core == member // ROW
    total = jnp.where(mine, near, far) + permuted(jnp.where(mine, far, near), CORE_SWAP)
    pieces = jnp.transpose(total.reshape(PLANES, per_plane, CHIPS, per_chip), (0, 2, 1, 3))
    pieces = pieces.reshape(PLANES * CHIPS, per_plane, per_chip)
    total = jnp.sum(exchanged(pieces, "blk", CORE_GROUPS), axis=0)
    held = lax.dynamic_slice(border_rhs, (plane * per_plane, core * per_core + chip * per_chip), (per_plane, per_chip))
    result = to_all(held - total, "blk", PLANES * CHIPS, CORE_GROUPS)
    result = result.reshape(PLANES, CHIPS, per_plane, per_chip)
    result = jnp.transpose(result, (0, 2, 1, 3)).reshape(rows, per_core)
    across = permuted(result, CORE_SWAP)
    return solved, jnp.concatenate([jnp.where(even, result, across), jnp.where(even, across, result)], axis=1)


def solution(mesh):
    placed = (
        P("blk", "rhs", None),
        P("blk", "rhs", None),
        P("rhs", "blk"),
        P("rhs", None),
        P("rhs", "blk"),
        P("rhs", None),
    )
    return jax.shard_map(
        body,
        mesh=mesh,
        in_specs=placed,
        out_specs=(P("rhs", "blk"), P("rhs", None)),
        check_vma=False,
    )
```

```python
import jax
import jax.numpy as jnp
from jax import lax
from jax.sharding import PartitionSpec as P

PLANES, CHIPS, CORES = 8, 4, 2
BLOCKS = PLANES * CHIPS * CORES
SHIFT = 4


def device(plane, chip, core):
    return (plane * CHIPS + chip) * CORES + core


CORE_SWAP = [(p, p ^ 1) for p in range(BLOCKS)]
TO_EVEN = [(p + 1, p) for p in range(0, BLOCKS, CORES)]
NEXT_CHIP = [(p, p + CORES) for p in range(BLOCKS - CORES)]
CORE_GROUPS = [[device(z, c, k) for z in range(PLANES) for c in range(CHIPS)] for k in range(CORES)]

ROW = 4
ROW_GROUPS = [[0, 1, 2, 3], [4, 5, 6, 7]]
ROW_SWAP = [(j, j ^ ROW) for j in range(2 * ROW)]


def product(left, right):
    return lax.dot_general(left, right, (((1,), (0,)), ((), ())), precision=lax.Precision.HIGH, preferred_element_type=jnp.float32)


def product_transposed(left, right):
    return lax.dot_general(left, right, (((1,), (1,)), ((), ())), precision=lax.Precision.HIGH, preferred_element_type=jnp.float32)


def exchanged(pieces, axis, groups=None):
    return lax.all_to_all(pieces, axis, 0, 0, axis_index_groups=groups)


def to_all(value, axis, count, groups=None):
    return exchanged(jnp.broadcast_to(value[None], (count,) + value.shape), axis, groups)


def permuted(value, pairs):
    return lax.ppermute(value, "blk", pairs)


def body(diag_inverse, coupling, rhs_t, prior, border_factor, border_rhs):
    rows, size = rhs_t.shape
    members = lax.axis_size("rhs")
    member = lax.axis_index("rhs")
    position = lax.axis_index("blk")
    core = position % CORES
    chip = (position // CORES) % CHIPS
    plane = position // (CORES * CHIPS)
    even = core == 0

    share = coupling.shape[1]
    gathered = to_all(jnp.concatenate([coupling[0], diag_inverse[0]], axis=0), "rhs", members)
    link = gathered[:, :share].reshape(size, size)
    inverse = gathered[:, share:].reshape(size, size)

    block_map = lax.dot_general(link, inverse, (((0,), (1,)), ((), ())), precision=lax.Precision.HIGH, preferred_element_type=jnp.float32)
    block_map = block_map * (-(2.0**-SHIFT))
    offset = product_transposed(rhs_t, inverse)
    offset = jnp.where(position == 0, offset + product(prior, block_map) * 2.0**SHIFT, offset)

    block = jnp.concatenate([block_map, offset], axis=0)
    other = permuted(block, CORE_SWAP)
    first, second = jnp.where(even, block, other), jnp.where(even, other, block)
    pair = product(first, second[:size])
    chip_map = pair[:size]
    chip_offset = pair[size:] * 2.0**SHIFT + second[size:]

    state = jnp.where(even, lax.dynamic_slice_in_dim(chip_map, member * rows, rows, 0), chip_offset)
    factor = jnp.where(even, 1.0, 2.0 ** (2 * SHIFT))
    added = jnp.where(even, 0.0, chip_offset)
    for _ in range(CHIPS - 2):
        state = product(permuted(state, NEXT_CHIP), chip_map) * factor + added
    state = permuted(state, NEXT_CHIP)
    across = permuted(state, CORE_SWAP)
    window = jnp.concatenate([jnp.where(even, state, across), jnp.where(even, across, state)], axis=0)
    window = product(window, jnp.where(even, block_map, chip_map))
    own_offset = window[rows:] * jnp.where(even, 2.0**SHIFT, 2.0 ** (2 * SHIFT)) + jnp.where(even, offset, chip_offset)
    scale = jnp.where(even, 2.0 ** (SHIFT * (2 * CHIPS - 1)), 2.0 ** (SHIFT * 2 * CHIPS))

    arrived = permuted(own_offset, [(device(0, c, 1), device(1, c, 1)) for c in range(CHIPS)])
    own_map = to_all(window[:rows], "rhs", members).reshape(size, size)
    own_map, copies = lax.optimization_barrier((own_map, jnp.broadcast_to(border_factor[None], (ROW,) + border_factor.shape)))
    border_near = exchanged(copies, "rhs", ROW_GROUPS)
    start = jnp.where(plane == 1, arrived, 0.0)
    for step in range(2, PLANES):
        end = product(start, own_map) * scale + own_offset
        arrived = permuted(end, [(device(step - 1, c, 1), device(step, c, 1)) for c in range(CHIPS)])
        if step == PLANES - 1:
            arrived, border_near = lax.optimization_barrier((arrived, border_near))
        start = jnp.where(plane == step, arrived, start)
    start = jnp.where(even, permuted(start, TO_EVEN), start)
    solved = product(start, own_map) * scale + own_offset

    border = border_rhs.shape[1]
    per_core, per_chip = border // CORES, border // CORES // CHIPS
    per_plane = rows // PLANES
    border_near = border_near.reshape(per_core, size)
    solved_across = lax.ppermute(solved, "rhs", ROW_SWAP)
    near = product_transposed(solved, border_near)
    far = lax.ppermute(product_transposed(solved_across, border_near), "rhs", ROW_SWAP)
    mine = core == member // ROW
    total = jnp.where(mine, near, far) + permuted(jnp.where(mine, far, near), CORE_SWAP)
    pieces = jnp.transpose(total.reshape(PLANES, per_plane, CHIPS, per_chip), (0, 2, 1, 3))
    pieces = pieces.reshape(PLANES * CHIPS, per_plane, per_chip)
    total = jnp.sum(exchanged(pieces, "blk", CORE_GROUPS), axis=0)
    held = lax.dynamic_slice(border_rhs, (plane * per_plane, core * per_core + chip * per_chip), (per_plane, per_chip))
    result = to_all(held - total, "blk", PLANES * CHIPS, CORE_GROUPS)
    result = result.reshape(PLANES, CHIPS, per_plane, per_chip)
    result = jnp.transpose(result, (0, 2, 1, 3)).reshape(rows, per_core)
    across = permuted(result, CORE_SWAP)
    return solved, jnp.concatenate([jnp.where(even, result, across), jnp.where(even, across, result)], axis=1)


def solution(mesh):
    placed = (
        P("blk", "rhs", None),
        P("blk", "rhs", None),
        P("rhs", "blk"),
        P("rhs", None),
        P("rhs", "blk"),
        P("rhs", None),
    )
    return jax.shard_map(
        body,
        mesh=mesh,
        in_specs=placed,
        out_specs=(P("rhs", "blk"), P("rhs", None)),
        check_vma=False,
    )
```

```python
import jax
import jax.numpy as jnp
from jax import lax
from jax.experimental import pallas as pl
from jax.experimental.pallas import tpu as pltpu
from jax.sharding import PartitionSpec as P

PLANES, CHIPS, CORES = 8, 4, 2
BLOCKS = PLANES * CHIPS * CORES
SHIFT = 4


def device(plane, chip, core):
    return (plane * CHIPS + chip) * CORES + core


CORE_SWAP = [(p, p ^ 1) for p in range(BLOCKS)]
TO_EVEN = [(p + 1, p) for p in range(0, BLOCKS, CORES)]
NEXT_CHIP = [(p, p + CORES) for p in range(BLOCKS - CORES)]
CORE_GROUPS = [[device(z, c, k) for z in range(PLANES) for c in range(CHIPS)] for k in range(CORES)]

ROW = 4
ROW_GROUPS = [[0, 1, 2, 3], [4, 5, 6, 7]]
ROW_SWAP = [(j, j ^ ROW) for j in range(2 * ROW)]


def product(left, right):
    return lax.dot_general(left, right, (((1,), (0,)), ((), ())), precision=lax.Precision.HIGH, preferred_element_type=jnp.float32)


def product_transposed(left, right):
    return lax.dot_general(left, right, (((1,), (1,)), ((), ())), precision=lax.Precision.HIGH, preferred_element_type=jnp.float32)


def split(value):
    high = value.astype(jnp.bfloat16)
    return high, (value - high.astype(jnp.float32)).astype(jnp.bfloat16)


def border_kernel(left_ref, border_ref, out_ref):
    left_high, left_low = split(left_ref[...])
    high, low = split(border_ref[...])

    def dot(left, right):
        return lax.dot_general(left, right, (((1,), (1,)), ((), ())), preferred_element_type=jnp.float32)

    out_ref[...] = dot(left_high, high) + (dot(left_high, low) + dot(left_low, high))


def border_product(left, border):
    rows, size = left.shape
    columns = border.shape[0]
    tile = columns // 4
    return pl.pallas_call(
        border_kernel,
        out_shape=jax.ShapeDtypeStruct((rows, columns), jnp.float32),
        grid=(columns // tile,),
        in_specs=[
            pl.BlockSpec((rows, size), lambda i: (0, 0)),
            pl.BlockSpec((tile, size), lambda i: (i, 0)),
        ],
        out_specs=pl.BlockSpec((rows, tile), lambda i: (0, i)),
        compiler_params=pltpu.CompilerParams(vmem_limit_bytes=8 * 2**20),
        cost_estimate=pl.CostEstimate(flops=6 * rows * size * columns, bytes_accessed=4 * size * columns, transcendentals=0),
    )(left, pltpu.with_memory_space_constraint(border, pltpu.HBM))


def exchanged(pieces, axis, groups=None):
    return lax.all_to_all(pieces, axis, 0, 0, axis_index_groups=groups)


def to_all(value, axis, count, groups=None):
    return exchanged(jnp.broadcast_to(value[None], (count,) + value.shape), axis, groups)


def permuted(value, pairs):
    return lax.ppermute(value, "blk", pairs)


def body(diag_inverse, coupling, rhs_t, prior, border_factor, border_rhs):
    rows, size = rhs_t.shape
    members = lax.axis_size("rhs")
    member = lax.axis_index("rhs")
    position = lax.axis_index("blk")
    core = position % CORES
    chip = (position // CORES) % CHIPS
    plane = position // (CORES * CHIPS)
    even = core == 0

    share = coupling.shape[1]
    gathered = to_all(jnp.concatenate([coupling[0], diag_inverse[0]], axis=0), "rhs", members)
    link = gathered[:, :share].reshape(size, size)
    inverse = gathered[:, share:].reshape(size, size)

    block_map = lax.dot_general(link, inverse, (((0,), (1,)), ((), ())), precision=lax.Precision.HIGH, preferred_element_type=jnp.float32)
    block_map = block_map * (-(2.0**-SHIFT))
    offset = product_transposed(rhs_t, inverse)
    offset = jnp.where(position == 0, offset + product(prior, block_map) * 2.0**SHIFT, offset)

    block = jnp.concatenate([block_map, offset], axis=0)
    other = permuted(block, CORE_SWAP)
    first, second = jnp.where(even, block, other), jnp.where(even, other, block)
    pair = product(first, second[:size])
    chip_map = pair[:size]
    chip_offset = pair[size:] * 2.0**SHIFT + second[size:]

    state = jnp.where(even, lax.dynamic_slice_in_dim(chip_map, member * rows, rows, 0), chip_offset)
    factor = jnp.where(even, 1.0, 2.0 ** (2 * SHIFT))
    added = jnp.where(even, 0.0, chip_offset)
    for _ in range(CHIPS - 2):
        state = product(permuted(state, NEXT_CHIP), chip_map) * factor + added
    state = permuted(state, NEXT_CHIP)
    across = permuted(state, CORE_SWAP)
    window = jnp.concatenate([jnp.where(even, state, across), jnp.where(even, across, state)], axis=0)
    window = product(window, jnp.where(even, block_map, chip_map))
    own_offset = window[rows:] * jnp.where(even, 2.0**SHIFT, 2.0 ** (2 * SHIFT)) + jnp.where(even, offset, chip_offset)
    scale = jnp.where(even, 2.0 ** (SHIFT * (2 * CHIPS - 1)), 2.0 ** (SHIFT * 2 * CHIPS))

    arrived = permuted(own_offset, [(device(0, c, 1), device(1, c, 1)) for c in range(CHIPS)])
    own_map = to_all(window[:rows], "rhs", members).reshape(size, size)
    own_map, copies = lax.optimization_barrier((own_map, jnp.broadcast_to(border_factor[None], (ROW,) + border_factor.shape)))
    border_near = exchanged(copies, "rhs", ROW_GROUPS)
    start = arrived
    for step in range(2, PLANES):
        end = product(start, own_map) * scale + own_offset
        arrived = permuted(end, [(device(step - 1, c, 1), device(step, c, 1)) for c in range(CHIPS)])
        if step == PLANES - 1:
            arrived, border_near = lax.optimization_barrier((arrived, border_near))
        start = start + arrived
    start = jnp.where(even, permuted(start, TO_EVEN), start)
    solved = product(start, own_map) * scale + own_offset

    border = border_rhs.shape[1]
    per_core, per_chip = border // CORES, border // CORES // CHIPS
    per_plane = rows // PLANES
    border_near = border_near.reshape(per_core, size)
    solved_across = lax.ppermute(solved, "rhs", ROW_SWAP)
    near = border_product(solved, border_near)
    far = lax.ppermute(border_product(solved_across, border_near), "rhs", ROW_SWAP)
    mine = core == member // ROW
    total = jnp.where(mine, near, far) + permuted(jnp.where(mine, far, near), CORE_SWAP)
    pieces = jnp.transpose(total.reshape(PLANES, per_plane, CHIPS, per_chip), (0, 2, 1, 3))
    pieces = pieces.reshape(PLANES * CHIPS, per_plane, per_chip)
    total = jnp.sum(exchanged(pieces, "blk", CORE_GROUPS), axis=0)
    held = lax.dynamic_slice(border_rhs, (plane * per_plane, core * per_core + chip * per_chip), (per_plane, per_chip))
    result = to_all(held - total, "blk", PLANES * CHIPS, CORE_GROUPS)
    result = result.reshape(PLANES, CHIPS, per_plane, per_chip)
    result = jnp.transpose(result, (0, 2, 1, 3)).reshape(rows, per_core)
    across = permuted(result, CORE_SWAP)
    return solved, jnp.concatenate([jnp.where(even, result, across), jnp.where(even, across, result)], axis=1)


def solution(mesh):
    placed = (
        P("blk", "rhs", None),
        P("blk", "rhs", None),
        P("rhs", "blk"),
        P("rhs", None),
        P("rhs", "blk"),
        P("rhs", None),
    )
    return jax.shard_map(
        body,
        mesh=mesh,
        in_specs=placed,
        out_specs=(P("rhs", "blk"), P("rhs", None)),
        check_vma=False,
    )
```

```python
import jax
import jax.numpy as jnp
from jax import lax
from jax.sharding import PartitionSpec as P

PLANES, CHIPS, CORES = 8, 4, 2
BLOCKS = PLANES * CHIPS * CORES
SHIFT = 4


def device(plane, chip, core):
    return (plane * CHIPS + chip) * CORES + core


CORE_SWAP = [(p, p ^ 1) for p in range(BLOCKS)]
TO_EVEN = [(device(z - 1, c, 1), device(z, c, 0)) for z in range(1, PLANES) for c in range(CHIPS)]
NEXT_CHIP = [(p, p + CORES) for p in range(BLOCKS - CORES)]
CORE_GROUPS = [[device(z, c, k) for z in range(PLANES) for c in range(CHIPS)] for k in range(CORES)]

ROW = 4
ROW_GROUPS = [[0, 1, 2, 3], [4, 5, 6, 7]]
ROW_SWAP = [(j, j ^ ROW) for j in range(2 * ROW)]


def product(left, right):
    return lax.dot_general(left, right, (((1,), (0,)), ((), ())), precision=lax.Precision.HIGH, preferred_element_type=jnp.float32)


def product_transposed(left, right):
    return lax.dot_general(left, right, (((1,), (1,)), ((), ())), precision=lax.Precision.HIGH, preferred_element_type=jnp.float32)


def exchanged(pieces, axis, groups=None):
    return lax.all_to_all(pieces, axis, 0, 0, axis_index_groups=groups)


def to_all(value, axis, count, groups=None):
    return exchanged(jnp.broadcast_to(value[None], (count,) + value.shape), axis, groups)


def permuted(value, pairs):
    return lax.ppermute(value, "blk", pairs)


def body(diag_inverse, coupling, rhs_t, prior, border_factor, border_rhs):
    rows, size = rhs_t.shape
    members = lax.axis_size("rhs")
    member = lax.axis_index("rhs")
    position = lax.axis_index("blk")
    core = position % CORES
    chip = (position // CORES) % CHIPS
    plane = position // (CORES * CHIPS)
    even = core == 0

    share = coupling.shape[1]
    gathered = to_all(jnp.concatenate([coupling[0], diag_inverse[0]], axis=0), "rhs", members)
    copies = jnp.broadcast_to(border_factor[None], (ROW,) + border_factor.shape)
    gathered, copies = lax.optimization_barrier((gathered, copies))
    link = gathered[:, :share].reshape(size, size)
    inverse = gathered[:, share:].reshape(size, size)

    block_map = lax.dot_general(link, inverse, (((0,), (1,)), ((), ())), precision=lax.Precision.HIGH, preferred_element_type=jnp.float32)
    block_map = block_map * (-(2.0**-SHIFT))
    offset = product_transposed(rhs_t, inverse)
    offset = jnp.where(position == 0, offset + product(prior, block_map) * 2.0**SHIFT, offset)

    block = jnp.concatenate([block_map, offset], axis=0)
    other = permuted(block, CORE_SWAP)
    first, second = jnp.where(even, block, other), jnp.where(even, other, block)
    pair = product(first, second[:size])
    chip_map = pair[:size]
    chip_offset = pair[size:] * 2.0**SHIFT + second[size:]

    state = jnp.where(even, lax.dynamic_slice_in_dim(chip_map, member * rows, rows, 0), chip_offset)
    factor = jnp.where(even, 1.0, 2.0 ** (2 * SHIFT))
    added = jnp.where(even, 0.0, chip_offset)
    for _ in range(CHIPS - 2):
        state = product(permuted(state, NEXT_CHIP), chip_map) * factor + added
    state = permuted(state, NEXT_CHIP)
    across = permuted(state, CORE_SWAP)
    window = jnp.concatenate([jnp.where(even, state, across), jnp.where(even, across, state)], axis=0)
    window = product(window, jnp.where(even, block_map, chip_map))
    own_offset = window[rows:] * jnp.where(even, 2.0**SHIFT, 2.0 ** (2 * SHIFT)) + jnp.where(even, offset, chip_offset)
    scale = jnp.where(even, 2.0 ** (SHIFT * (2 * CHIPS - 1)), 2.0 ** (SHIFT * 2 * CHIPS))

    arrived = permuted(own_offset, [(device(0, c, 1), device(1, c, 1)) for c in range(CHIPS)])
    own_map = to_all(window[:rows], "rhs", members).reshape(size, size)
    own_map, copies = lax.optimization_barrier((own_map, copies))
    border_near = exchanged(copies, "rhs", ROW_GROUPS)
    start = arrived
    for step in range(2, PLANES):
        end = product(start, own_map) * scale + own_offset
        arrived = permuted(end, [(device(step - 1, c, 1), device(step, c, 1)) for c in range(CHIPS)])
        if step == PLANES - 1:
            arrived, border_near = lax.optimization_barrier((arrived, border_near))
        start = start + arrived
    start = jnp.where(even, permuted(end, TO_EVEN), start)
    solved = product(start, own_map) * scale + own_offset

    border = border_rhs.shape[1]
    per_core, per_chip = border // CORES, border // CORES // CHIPS
    per_plane = rows // PLANES
    border_near = border_near.reshape(per_core, size)
    solved_across = lax.ppermute(solved, "rhs", ROW_SWAP)
    near = product_transposed(solved, border_near)
    far = lax.ppermute(product_transposed(solved_across, border_near), "rhs", ROW_SWAP)
    mine = core == member // ROW
    total = jnp.where(mine, near, far) + permuted(jnp.where(mine, far, near), CORE_SWAP)
    pieces = jnp.transpose(total.reshape(PLANES, per_plane, CHIPS, per_chip), (0, 2, 1, 3))
    pieces = pieces.reshape(PLANES * CHIPS, per_plane, per_chip)
    total = jnp.sum(exchanged(pieces, "blk", CORE_GROUPS), axis=0)
    held = lax.dynamic_slice(border_rhs, (plane * per_plane, core * per_core + chip * per_chip), (per_plane, per_chip))
    result = to_all(held - total, "blk", PLANES * CHIPS, CORE_GROUPS)
    result = result.reshape(PLANES, CHIPS, per_plane, per_chip)
    result = jnp.transpose(result, (0, 2, 1, 3)).reshape(rows, per_core)
    across = permuted(result, CORE_SWAP)
    return solved, jnp.concatenate([jnp.where(even, result, across), jnp.where(even, across, result)], axis=1)


def solution(mesh):
    placed = (
        P("blk", "rhs", None),
        P("blk", "rhs", None),
        P("rhs", "blk"),
        P("rhs", None),
        P("rhs", "blk"),
        P("rhs", None),
    )
    return jax.shard_map(
        body,
        mesh=mesh,
        in_specs=placed,
        out_specs=(P("rhs", "blk"), P("rhs", None)),
        check_vma=False,
    )
```

```python
import jax
import jax.numpy as jnp
from jax import lax
from jax.sharding import PartitionSpec as P

PLANES, CHIPS, CORES = 8, 4, 2
BLOCKS = PLANES * CHIPS * CORES
SHIFT = 4


def device(plane, chip, core):
    return (plane * CHIPS + chip) * CORES + core


CORE_SWAP = [(p, p ^ 1) for p in range(BLOCKS)]
TO_EVEN = [(device(z - 1, c, 1), device(z, c, 0)) for z in range(1, PLANES) for c in range(CHIPS)]
NEXT_CHIP = [(p, p + CORES) for p in range(BLOCKS - CORES)]
CORE_GROUPS = [[device(z, c, k) for z in range(PLANES) for c in range(CHIPS)] for k in range(CORES)]

ROW = 4
ROW_GROUPS = [[0, 1, 2, 3], [4, 5, 6, 7]]
ROW_SWAP = [(j, j ^ ROW) for j in range(2 * ROW)]


def across_pairs(core):
    members = 2 * ROW
    return [
        (device(z - 1, c, 1) * members + j, device(z, c, core) * members + (j ^ ROW))
        for z in range(1, PLANES)
        for c in range(CHIPS)
        for j in range(members)
    ]


def product(left, right):
    return lax.dot_general(left, right, (((1,), (0,)), ((), ())), precision=lax.Precision.HIGH, preferred_element_type=jnp.float32)


def product_transposed(left, right):
    return lax.dot_general(left, right, (((1,), (1,)), ((), ())), precision=lax.Precision.HIGH, preferred_element_type=jnp.float32)


def exchanged(pieces, axis, groups=None):
    return lax.all_to_all(pieces, axis, 0, 0, axis_index_groups=groups)


def to_all(value, axis, count, groups=None):
    return exchanged(jnp.broadcast_to(value[None], (count,) + value.shape), axis, groups)


def permuted(value, pairs):
    return lax.ppermute(value, "blk", pairs)


def body(diag_inverse, coupling, rhs_t, prior, border_factor, border_rhs):
    rows, size = rhs_t.shape
    members = lax.axis_size("rhs")
    member = lax.axis_index("rhs")
    position = lax.axis_index("blk")
    core = position % CORES
    chip = (position // CORES) % CHIPS
    plane = position // (CORES * CHIPS)
    even = core == 0

    share = coupling.shape[1]
    gathered = to_all(jnp.concatenate([coupling[0], diag_inverse[0]], axis=0), "rhs", members)
    copies = jnp.broadcast_to(border_factor[None], (ROW,) + border_factor.shape)
    gathered, copies = lax.optimization_barrier((gathered, copies))
    link = gathered[:, :share].reshape(size, size)
    inverse = gathered[:, share:].reshape(size, size)

    block_map = lax.dot_general(link, inverse, (((0,), (1,)), ((), ())), precision=lax.Precision.HIGH, preferred_element_type=jnp.float32)
    block_map = block_map * (-(2.0**-SHIFT))
    offset = product_transposed(rhs_t, inverse)
    offset = jnp.where(position == 0, offset + product(prior, block_map) * 2.0**SHIFT, offset)

    block = jnp.concatenate([block_map, offset], axis=0)
    other = permuted(block, CORE_SWAP)
    first, second = jnp.where(even, block, other), jnp.where(even, other, block)
    pair = product(first, second[:size])
    chip_map = pair[:size]
    chip_offset = pair[size:] * 2.0**SHIFT + second[size:]

    state = jnp.where(even, lax.dynamic_slice_in_dim(chip_map, member * rows, rows, 0), chip_offset)
    factor = jnp.where(even, 1.0, 2.0 ** (2 * SHIFT))
    added = jnp.where(even, 0.0, chip_offset)
    for _ in range(CHIPS - 2):
        state = product(permuted(state, NEXT_CHIP), chip_map) * factor + added
    state = permuted(state, NEXT_CHIP)
    across = permuted(state, CORE_SWAP)
    window = jnp.concatenate([jnp.where(even, state, across), jnp.where(even, across, state)], axis=0)
    window = product(window, jnp.where(even, block_map, chip_map))
    own_offset = window[rows:] * jnp.where(even, 2.0**SHIFT, 2.0 ** (2 * SHIFT)) + jnp.where(even, offset, chip_offset)
    scale = jnp.where(even, 2.0 ** (SHIFT * (2 * CHIPS - 1)), 2.0 ** (SHIFT * 2 * CHIPS))

    arrived = permuted(own_offset, [(device(0, c, 1), device(1, c, 1)) for c in range(CHIPS)])
    own_map = to_all(window[:rows], "rhs", members).reshape(size, size)
    offset_across = lax.ppermute(own_offset, "rhs", ROW_SWAP)
    own_map, copies, offset_across = lax.optimization_barrier((own_map, copies, offset_across))
    border_near = exchanged(copies, "rhs", ROW_GROUPS)
    start = arrived
    for step in range(2, PLANES):
        end = product(start, own_map) * scale + own_offset
        arrived = permuted(end, [(device(step - 1, c, 1), device(step, c, 1)) for c in range(CHIPS)])
        if step == PLANES - 1:
            arrived, border_near = lax.optimization_barrier((arrived, border_near))
        start = start + arrived
    start = jnp.where(even, permuted(end, TO_EVEN), start)
    start_across = lax.ppermute(end, ("blk", "rhs"), across_pairs(0)) + lax.ppermute(end, ("blk", "rhs"), across_pairs(1))
    solved = product(start, own_map) * scale + own_offset
    solved_across = product(start_across, own_map) * scale + offset_across

    border = border_rhs.shape[1]
    per_core, per_chip = border // CORES, border // CORES // CHIPS
    per_plane = rows // PLANES
    border_near = border_near.reshape(per_core, size)
    near = product_transposed(solved, border_near)
    far = lax.ppermute(product_transposed(solved_across, border_near), "rhs", ROW_SWAP)
    mine = core == member // ROW
    total = jnp.where(mine, near, far) + permuted(jnp.where(mine, far, near), CORE_SWAP)
    pieces = jnp.transpose(total.reshape(PLANES, per_plane, CHIPS, per_chip), (0, 2, 1, 3))
    pieces = pieces.reshape(PLANES * CHIPS, per_plane, per_chip)
    total = jnp.sum(exchanged(pieces, "blk", CORE_GROUPS), axis=0)
    held = lax.dynamic_slice(border_rhs, (plane * per_plane, core * per_core + chip * per_chip), (per_plane, per_chip))
    result = to_all(held - total, "blk", PLANES * CHIPS, CORE_GROUPS)
    result = result.reshape(PLANES, CHIPS, per_plane, per_chip)
    result = jnp.transpose(result, (0, 2, 1, 3)).reshape(rows, per_core)
    across = permuted(result, CORE_SWAP)
    return solved, jnp.concatenate([jnp.where(even, result, across), jnp.where(even, across, result)], axis=1)


def solution(mesh):
    placed = (
        P("blk", "rhs", None),
        P("blk", "rhs", None),
        P("rhs", "blk"),
        P("rhs", None),
        P("rhs", "blk"),
        P("rhs", None),
    )
    return jax.shard_map(
        body,
        mesh=mesh,
        in_specs=placed,
        out_specs=(P("rhs", "blk"), P("rhs", None)),
        check_vma=False,
    )
```

```python
import jax
import jax.numpy as jnp
from jax import lax
from jax.sharding import PartitionSpec as P

PLANES, CHIPS, CORES = 8, 4, 2
BLOCKS = PLANES * CHIPS * CORES
SHIFT = 4


def device(plane, chip, core):
    return (plane * CHIPS + chip) * CORES + core


CORE_SWAP = [(p, p ^ 1) for p in range(BLOCKS)]
TO_EVEN = [(device(z - 1, c, 1), device(z, c, 0)) for z in range(1, PLANES) for c in range(CHIPS)]
NEXT_CHIP = [(p, p + CORES) for p in range(BLOCKS - CORES)]
CORE_GROUPS = [[device(z, c, k) for z in range(PLANES) for c in range(CHIPS)] for k in range(CORES)]

ROW = 4
ROW_GROUPS = [[0, 1, 2, 3], [4, 5, 6, 7]]
ROW_SWAP = [(j, j ^ ROW) for j in range(2 * ROW)]


def across_pairs(core):
    members = 2 * ROW
    return [
        (device(z - 1, c, 1) * members + j, device(z, c, core) * members + (j ^ ROW))
        for z in range(1, PLANES)
        for c in range(CHIPS)
        for j in range(members)
    ]


def product(left, right):
    return lax.dot_general(left, right, (((1,), (0,)), ((), ())), precision=lax.Precision.HIGH, preferred_element_type=jnp.float32)


def product_transposed(left, right):
    return lax.dot_general(left, right, (((1,), (1,)), ((), ())), precision=lax.Precision.HIGH, preferred_element_type=jnp.float32)


def exchanged(pieces, axis, groups=None):
    return lax.all_to_all(pieces, axis, 0, 0, axis_index_groups=groups)


def to_all(value, axis, count, groups=None):
    return exchanged(jnp.broadcast_to(value[None], (count,) + value.shape), axis, groups)


def permuted(value, pairs):
    return lax.ppermute(value, "blk", pairs)


def body(diag_inverse, coupling, rhs_t, prior, border_factor, border_rhs):
    rows, size = rhs_t.shape
    members = lax.axis_size("rhs")
    member = lax.axis_index("rhs")
    position = lax.axis_index("blk")
    core = position % CORES
    chip = (position // CORES) % CHIPS
    plane = position // (CORES * CHIPS)
    even = core == 0

    share = coupling.shape[1]
    gathered = exchanged(
        jnp.concatenate([jnp.broadcast_to(part, (members,) + part.shape[1:]) for part in (coupling, diag_inverse)], axis=1), "rhs"
    )
    copies = jnp.broadcast_to(border_factor[None], (ROW,) + border_factor.shape)
    gathered, copies = lax.optimization_barrier((gathered, copies))
    link = gathered[:, :share].reshape(size, size)
    inverse = gathered[:, share:].reshape(size, size)

    block_map = lax.dot_general(link, inverse, (((0,), (1,)), ((), ())), precision=lax.Precision.HIGH, preferred_element_type=jnp.float32)
    block_map = block_map * (-(2.0**-SHIFT))
    offset = product_transposed(rhs_t, inverse)
    offset = jnp.where(position == 0, offset + product(prior, block_map) * 2.0**SHIFT, offset)

    block = jnp.concatenate([block_map, offset], axis=0)
    other = permuted(block, CORE_SWAP)
    first, second = jnp.where(even, block, other), jnp.where(even, other, block)
    pair = product(first, second[:size])
    chip_map = pair[:size]
    chip_offset = pair[size:] * 2.0**SHIFT + second[size:]

    state = jnp.where(even, lax.dynamic_slice_in_dim(chip_map, member * rows, rows, 0), chip_offset)
    factor = jnp.where(even, 1.0, 2.0 ** (2 * SHIFT))
    added = jnp.where(even, 0.0, chip_offset)
    for _ in range(CHIPS - 2):
        state = product(permuted(state, NEXT_CHIP), chip_map) * factor + added
    state = permuted(state, NEXT_CHIP)
    across = permuted(state, CORE_SWAP)
    window = jnp.concatenate([jnp.where(even, state, across), jnp.where(even, across, state)], axis=0)
    window = product(window, jnp.where(even, block_map, chip_map))
    own_offset = window[rows:] * jnp.where(even, 2.0**SHIFT, 2.0 ** (2 * SHIFT)) + jnp.where(even, offset, chip_offset)
    scale = jnp.where(even, 2.0 ** (SHIFT * (2 * CHIPS - 1)), 2.0 ** (SHIFT * 2 * CHIPS))

    arrived = permuted(own_offset, [(device(0, c, 1), device(1, c, 1)) for c in range(CHIPS)])
    own_map = to_all(window[:rows], "rhs", members).reshape(size, size)
    offset_across = lax.ppermute(own_offset, "rhs", ROW_SWAP)
    own_map, copies, offset_across = lax.optimization_barrier((own_map, copies, offset_across))
    border_near = exchanged(copies, "rhs", ROW_GROUPS)
    start = arrived
    for step in range(2, PLANES):
        end = product(start, own_map) * scale + own_offset
        arrived = permuted(end, [(device(step - 1, c, 1), device(step, c, 1)) for c in range(CHIPS)])
        if step == PLANES - 1:
            arrived, border_near = lax.optimization_barrier((arrived, border_near))
        start = start + arrived
    start = jnp.where(even, permuted(end, TO_EVEN), start)
    start_across = lax.ppermute(end, ("blk", "rhs"), across_pairs(0)) + lax.ppermute(end, ("blk", "rhs"), across_pairs(1))
    solved = product(start, own_map) * scale + own_offset
    solved_across = product(start_across, own_map) * scale + offset_across

    border = border_rhs.shape[1]
    per_core, per_chip = border // CORES, border // CORES // CHIPS
    per_plane = rows // PLANES
    border_near = border_near.reshape(per_core, size)
    near = product_transposed(solved, border_near)
    far = lax.ppermute(product_transposed(solved_across, border_near), "rhs", ROW_SWAP)
    mine = core == member // ROW
    total = jnp.where(mine, near, far) + permuted(jnp.where(mine, far, near), CORE_SWAP)
    pieces = jnp.transpose(total.reshape(PLANES, per_plane, CHIPS, per_chip), (0, 2, 1, 3))
    pieces = pieces.reshape(PLANES * CHIPS, per_plane, per_chip)
    total = jnp.sum(exchanged(pieces, "blk", CORE_GROUPS), axis=0)
    held = lax.dynamic_slice(border_rhs, (plane * per_plane, core * per_core + chip * per_chip), (per_plane, per_chip))
    result = to_all(held - total, "blk", PLANES * CHIPS, CORE_GROUPS)
    result = result.reshape(PLANES, CHIPS, per_plane, per_chip)
    result = jnp.transpose(result, (0, 2, 1, 3)).reshape(rows, per_core)
    across = permuted(result, CORE_SWAP)
    return solved, jnp.concatenate([jnp.where(even, result, across), jnp.where(even, across, result)], axis=1)


def solution(mesh):
    placed = (
        P("blk", "rhs", None),
        P("blk", "rhs", None),
        P("rhs", "blk"),
        P("rhs", None),
        P("rhs", "blk"),
        P("rhs", None),
    )
    return jax.shard_map(
        body,
        mesh=mesh,
        in_specs=placed,
        out_specs=(P("rhs", "blk"), P("rhs", None)),
        check_vma=False,
    )
```
